32 devices in a mesh: rows: 4 (over y, x), cols: 8 (over z, core).
Axes of the slice: x: 2, y: 2, z: 4, core: 2. Of those that a mesh axis runs over, the one named last changes fastest.
Arguments:
- c_eta: float32 [512, 2048], P('rows', 'cols'), may hold values from -4 to 4
- c_flux: float32 [2, 512, 2048], P(None, 'rows', 'cols'), may hold values from -150 to 150
- c_depth: float32 [512, 2048], P('rows', 'cols'), may hold values from 100 to 4000
- f_bed: float32 [128, 2048], P('rows', 'cols'), may hold values from -3 to 1
- f_depth: float32 [128, 2048], P('rows', 'cols'), may hold values from 0.05 to 3
- f_wet: int32 [128, 2048], P('rows', 'cols'), may hold values 0 or 1
- f_class: int32 [128, 2048], P('rows', 'cols'), may hold values from 0 to 10
- manning: float32 [11], replicated, may hold values from 0.02 to 0.2
- nest_map: int32 [2048], replicated, may hold values from 0 to 1048575, as said below
Outputs:
- c_eta_out: float32 [512, 2048], P('rows', 'cols')
- f_water: float32 [128, 2048], P('rows', 'cols')
- f_flux: float32 [2, 128, 2048], P(None, 'rows', 'cols')
The draws below stay inside these ranges and needn't reach their ends.
Inputs may be any that keep to these rules, and one draw needn't show every extreme that they name: `nest_map`: entry b is the flat index, row times 2048 plus column, of the coarse cell that drives fine boundary cell b; entries with the same b // 18 are equal; for s = b // 18 the coarse row lies in [(s * 128) % 512, (s * 128) % 512 + 128) and the coarse column is min(s * 18 * 1 + 256 + j, 2047) for some j in 0..128.
All inputs are finite; a program needn't handle non-finite values. No bound on the sum of `f_wet` on one device may be relied on, other than what follows from the above.
Results may differ from the reference program's by a relative error of at most 0.00002.
Values sent between devices are 32-bit elements; how exact they have to be, the bound alone decides.
A program may use at most 64 MiB of HBM per device.

```python
import math
import jax
import jax.numpy as jnp

CR = 128
CC = 256
NCLASS = 11
RATIO = 18
CSTEPS = 2
SUB = 3
FSTEPS = 6
NFR = 128
NFC = 2048
CROWS = 512
CCOLS = 2048
NB = 2048


def draw_nest_map(key, part):
    segments = (NB + RATIO - 1) // RATIO
    row_key = jax.random.fold_in(key, 11)
    col_key = jax.random.fold_in(key, 23)
    seg_index = jnp.arange(segments, dtype=jnp.int32)
    row_base = seg_index * CR % CROWS
    coarse_row = row_base + jax.random.randint(row_key, (segments,), 0, CR)
    col_base = seg_index * RATIO * CCOLS // NB + CC
    coarse_col = jnp.minimum(col_base + jax.random.randint(col_key, (segments,), 0, CC // 2 + 1), CCOLS - 1)
    cells = coarse_row * CCOLS + coarse_col
    return jnp.repeat(cells, RATIO, total_repeat_length=NB).astype(jnp.int32)


def plant(values, key, least, top_value):
    place = [jax.random.randint(jax.random.fold_in(key, axis), (), 0, length) for axis, length in enumerate(values.shape)]
    longest = values.shape.index(max(values.shape))
    neighbour = place[:longest] + [(place[longest] + 1) % values.shape[longest]] + place[longest + 1:]
    return values.at[tuple(place)].set(least).at[tuple(neighbour)].set(top_value)


def block_scale(key, dims, pieces, smallest, largest):
    gain, own = 1.0, jax.random.fold_in(key, 6)
    for dim, blocks in pieces:
        heights = jnp.exp(jax.random.uniform(jax.random.fold_in(own, dim), (blocks,), jnp.float32, smallest / len(pieces), largest / len(pieces)))
        gain = gain * jnp.repeat(heights, dims[dim] // blocks).reshape([-1 if axis == dim else 1 for axis in range(len(dims))])
    return gain


def scatter_about(rng, extent, deviation, limit, pieces=(), kind=jnp.bfloat16):
    entries = jax.random.normal(rng, extent, jnp.float32) * deviation
    if len(pieces) > 0:
        entries = block_scale(rng, extent, pieces, -0.22, 0.18) * entries
    return jnp.clip(entries, min=-limit, max=limit).astype(kind)


def setup_inputs(seed: int = 0) -> dict:
    seeds = jax.random.split(jax.random.key(seed), 10)
    c_eta = scatter_about(seeds[0], (CROWS, CCOLS), 1.0, 4.0, ((0, 4), (1, 8)), jnp.float32)
    c_flux = jnp.clip(jax.random.uniform(seeds[1], (2, CROWS, CCOLS), jnp.float32, -150.0, 150.0) * block_scale(seeds[1], (2, CROWS, CCOLS), ((1, 4), (2, 8)), -0.4, 0.0), -150.0, 150.0)
    c_depth = jnp.clip(jnp.exp(math.log(4000.0) - 3.6888795 * jax.random.uniform(seeds[2], (CROWS, CCOLS), jnp.float32) ** block_scale(seeds[2], (CROWS, CCOLS), ((0, 4), (1, 8)), -0.2, 0.2)), 100.0, 4000.0)
    f_bed = jnp.clip(-3.0 + 4.0 * jax.random.uniform(seeds[3], (NFR, NFC), jnp.float32) ** block_scale(seeds[3], (NFR, NFC), ((0, 4), (1, 8)), -0.2, 0.2), -3.0, 1.0)
    f_depth = jnp.clip(jnp.exp(math.log(3.0) - 4.0943445 * jax.random.uniform(seeds[4], (NFR, NFC), jnp.float32) ** block_scale(seeds[4], (NFR, NFC), ((0, 4), (1, 8)), -0.2, 0.2)), 0.05, 3.0)
    f_wet = plant((jax.random.randint(seeds[5], (NFR, NFC), 0, 5) < 3).astype(jnp.int32), jax.random.fold_in(seeds[5], 1), 0, 1)
    f_class = plant(jax.random.randint(seeds[6], (NFR, NFC), 0, NCLASS), jax.random.fold_in(seeds[6], 1), 0, NCLASS - 1).astype(jnp.int32)
    manning = jnp.clip(jnp.exp(jax.random.uniform(seeds[7], (NCLASS,), jnp.float32, math.log(0.02), math.log(0.2))), 0.02, 0.2)
    nest_map = draw_nest_map(jax.random.fold_in(seeds[9], 71), 0)
    return dict(c_eta=c_eta, c_flux=c_flux, c_depth=c_depth, f_bed=f_bed, f_depth=f_depth, f_wet=f_wet, f_class=f_class, manning=manning, nest_map=nest_map)


gravity = 9.81
coarse_spacing = 90.0
coarse_tick = 0.25
fine_spacing = 5.0
depth_floor = 0.01
dry_depth = 0.05

def coarse_update(padded):
    surf = padded[0]
    total = padded[1]
    rows_flux = padded[2]
    cols_flux = padded[3]
    face_rows = jnp.minimum(total[:-1, 1:-1], total[1:, 1:-1])
    new_rows = jnp.minimum(face_rows, 1.0) * (rows_flux[:-1, 1:-1] - coarse_tick * gravity * face_rows * (surf[1:, 1:-1] - surf[:-1, 1:-1]) / coarse_spacing)
    face_cols = jnp.minimum(total[1:-1, :-1], total[1:-1, 1:])
    new_cols = jnp.minimum(face_cols, 1.0) * (cols_flux[1:-1, :-1] - coarse_tick * gravity * face_cols * (surf[1:-1, 1:] - surf[1:-1, :-1]) / coarse_spacing)
    surface = surf[1:-1, 1:-1] - coarse_tick / coarse_spacing * (new_rows[1:] - new_rows[:-1] + (new_cols[:, 1:] - new_cols[:, :-1]))
    return (surface, new_rows[1:], new_cols[:, 1:])

def face_flux(flux_old, face_depth, slope, rough, fine_tick):
    wetness = jnp.minimum(face_depth / dry_depth, 1.0)
    driven = flux_old - fine_tick * gravity * face_depth * slope / fine_spacing
    friction = 1.0 + fine_tick * gravity * rough * rough * jnp.abs(flux_old) / jnp.power(jnp.maximum(face_depth, depth_floor), 7.0 / 3.0)
    return wetness * driven / friction

def fine_faces(water_pad, bed_pad, rough_pad, rows_pad, cols_pad, fine_tick):
    surf = bed_pad + water_pad
    depth_rows = jnp.maximum(jnp.maximum(surf[:-1, 1:-1], surf[1:, 1:-1]) - jnp.maximum(bed_pad[:-1, 1:-1], bed_pad[1:, 1:-1]), 0.0)
    rough_rows = 0.5 * (rough_pad[:-1, 1:-1] + rough_pad[1:, 1:-1])
    new_rows = face_flux(rows_pad[:-1, 1:-1], depth_rows, surf[1:, 1:-1] - surf[:-1, 1:-1], rough_rows, fine_tick)
    depth_cols = jnp.maximum(jnp.maximum(surf[1:-1, :-1], surf[1:-1, 1:]) - jnp.maximum(bed_pad[1:-1, :-1], bed_pad[1:-1, 1:]), 0.0)
    rough_cols = 0.5 * (rough_pad[1:-1, :-1] + rough_pad[1:-1, 1:])
    new_cols = face_flux(cols_pad[1:-1, :-1], depth_cols, surf[1:-1, 1:] - surf[1:-1, :-1], rough_cols, fine_tick)
    return (new_rows, new_cols)

def open_boundary(water_top, bed_top, bnd_surface, bnd_velocity):
    return water_top * bnd_velocity + jnp.sqrt(gravity * jnp.maximum(water_top, depth_floor)) * (bnd_surface - (bed_top + water_top))

def blend(levels_stack, fine_index):
    lower = fine_index // SUB
    weight = (fine_index % SUB + 1) / SUB
    return (1.0 - weight) * levels_stack[lower] + weight * levels_stack[lower + 1]

def reference(c_eta, c_flux, c_depth, f_bed, f_depth, f_wet, f_class, manning, nest_map):
    surface = c_eta
    rows_flux = c_flux[0]
    cols_flux = c_flux[1]
    sampled = [jnp.stack([surface.reshape(-1)[nest_map], (rows_flux / (c_depth + surface)).reshape(-1)[nest_map]])]
    for coarse_index in range(CSTEPS):
        stacked = jnp.stack([surface, c_depth + surface, rows_flux, cols_flux])
        padded = jnp.pad(stacked, ((0, 0), (1, 1), (1, 1)))
        surface, rows_flux, cols_flux = coarse_update(padded)
        sampled.append(jnp.stack([surface.reshape(-1)[nest_map], (rows_flux / (c_depth + surface)).reshape(-1)[nest_map]]))
    levels_stack = jnp.stack(sampled)
    roughness = manning[f_class]
    water = f_wet.astype(f_bed.dtype) * f_depth
    fine_rows = jnp.zeros_like(water)
    fine_cols = jnp.zeros_like(water)
    bed_pad = jnp.pad(f_bed, 1)
    rough_pad = jnp.pad(roughness, 1)
    fine_tick = coarse_tick / SUB
    row_faces = jnp.arange(NFR + 1)
    row_keep = jnp.where(row_faces == NFR, 0.0, 1.0)[:, None]
    col_faces = jnp.arange(NFC + 1)
    col_keep = jnp.where((col_faces == 0) | (col_faces == NFC), 0.0, 1.0)[None, :]
    for fine_index in range(FSTEPS):
        bnd = blend(levels_stack, fine_index)
        water_pad = jnp.pad(water, 1)
        new_rows, new_cols = fine_faces(water_pad, bed_pad, rough_pad, jnp.pad(fine_rows, 1), jnp.pad(fine_cols, 1), fine_tick)
        new_rows = new_rows * row_keep
        new_cols = new_cols * col_keep
        top_flux = open_boundary(water_pad[1, 1:-1], bed_pad[1, 1:-1], bnd[0], bnd[1])
        new_rows = jnp.concatenate([top_flux[None, :], new_rows[1:]], axis=0)
        water = water_pad[1:-1, 1:-1] - fine_tick / fine_spacing * (new_rows[1:] - new_rows[:-1] + (new_cols[:, 1:] - new_cols[:, :-1]))
        fine_rows = new_rows[1:]
        fine_cols = new_cols[:, 1:]
    return (surface, water, jnp.stack([fine_rows, fine_cols]))
```

```python
import functools

import jax
import jax.numpy as jnp
from jax import lax
from jax.experimental import pallas as pl
from jax.experimental.pallas import tpu as pltpu
from jax.sharding import PartitionSpec as P

NCLASS = 11
SUB = 3
FSTEPS = 6
RATIO = 18
REACH = 128

gravity = 9.81
coarse_spacing = 90.0
coarse_tick = 0.25
fine_spacing = 5.0
depth_floor = 0.01
dry_depth = 0.05
fine_tick = coarse_tick / SUB

LANES = 128
PAD = 8
MESH = pl.DeviceIdType.MESH


def turn(x, shift, axis):
    return pltpu.roll(x, shift % x.shape[axis], axis)


def coarse_step(surf, depth, rows_flux, cols_flux):
    total = depth + surf

    def face(flux, axis):
        d = jnp.minimum(total, turn(total, -1, axis))
        slope = turn(surf, -1, axis) - surf
        return jnp.minimum(d, 1.0) * (flux - (coarse_tick * gravity / coarse_spacing) * d * slope)

    new_rows = face(rows_flux, 0)
    new_cols = face(cols_flux, 1)
    surf = surf - (coarse_tick / coarse_spacing) * (
        new_rows - turn(new_rows, 1, 0) + (new_cols - turn(new_cols, 1, 1))
    )
    return surf, new_rows, new_cols


def fine_run(water, bed, rough, row_keep, col_keep, top):
    bed_faces = [jnp.maximum(bed, turn(bed, -1, axis)) for axis in (0, 1)]
    drag = []
    for axis in (0, 1):
        n = 0.5 * (rough + turn(rough, -1, axis))
        drag.append((fine_tick * gravity) * n * n)
    keep = (row_keep, col_keep)
    flux = [None, None]
    first_row = lax.broadcasted_iota(jnp.int32, water.shape, 0) == 0
    for step in range(FSTEPS):
        surf = bed + water
        new = []
        for axis in (0, 1):
            after = turn(surf, -1, axis)
            d = jnp.maximum(jnp.maximum(surf, after) - bed_faces[axis], 0.0)
            push = (fine_tick * gravity / fine_spacing) * d * (after - surf)
            wet = jnp.minimum(d * (1.0 / dry_depth), 1.0)
            if step == 0:
                value = wet * (-push)
            else:
                power = jnp.exp((-7.0 / 3.0) * jnp.log(jnp.maximum(d, depth_floor)))
                friction = 1.0 + drag[axis] * jnp.abs(flux[axis]) * power
                value = wet * (flux[axis] - push) / friction
            if keep[axis] is not None:
                value = jnp.where(keep[axis], value, 0.0)
            new.append(value)
        above = turn(new[0], 1, 0)
        if top is not None:
            above = jnp.where(first_row, top(step, water[0:1, :], bed[0:1, :]), above)
        water = water - (fine_tick / fine_spacing) * (new[0] - above + (new[1] - turn(new[1], 1, 1)))
        flux = new
    return water, flux[0], flux[1]


def kernel(
    nrow, ncol, nslots,
    eta_ref, flux_ref, depth_ref, bed_ref, fdepth_ref, wet_ref, class_ref, manning_ref, nest_ref,
    out_eta, out_water, out_flux,
    ce, cs, pc, cl, cr, fe, pf, fl, fr, samp, sbuf, rbuf, acc,
    send_sem, recv_sem, ssend_sem, srecv_sem,
):
    r = lax.axis_index("rows")
    c = lax.axis_index("cols")
    th, tw = eta_ref.shape
    fh = bed_ref.shape[0]
    nb = nest_ref.shape[0]
    width = tw * ncol
    up, dn = r > 0, r < nrow - 1
    lf, rt = c > 0, c < ncol - 1
    around = [
        (up, r - 1, c), (dn, r + 1, c), (lf, r, c - 1), (rt, r, c + 1),
        (up & lf, r - 1, c - 1), (up & rt, r - 1, c + 1),
        (dn & lf, r + 1, c - 1), (dn & rt, r + 1, c + 1),
    ]
    arrives = [dn, up, rt, lf, dn & rt, dn & lf, up & rt, up & lf]

    barrier = pltpu.get_barrier_semaphore()
    expected = jnp.int32(0)
    for there, rr, cc in around:
        @pl.when(there)
        def _(rr=rr, cc=cc):
            pl.semaphore_signal(barrier, inc=1, device_id=(rr, cc), device_id_type=MESH)
        expected = expected + there.astype(jnp.int32)

    @pl.when(r == 0)
    def _():
        for k in range(3):
            for rr in range(nrow):
                if k == 0 and rr == 0:
                    continue

                @pl.when(c + k < ncol)
                def _(k=k, rr=rr):
                    pl.semaphore_signal(barrier, inc=1, device_id=(rr, c + k), device_id_type=MESH)

    for k in range(3):
        sends = c - k >= 0
        if k == 0:
            sends = r > 0
        expected = expected + sends.astype(jnp.int32)

    def copies(ext, packed, left, right, high, base):
        a, b = PAD, PAD + high
        whole = [
            (ext.at[:, a:a + PAD, 0:tw], ext.at[:, b:b + PAD, 0:tw]),
            (ext.at[:, b - PAD:b, 0:tw], ext.at[:, 0:a, 0:tw]),
            (packed, right.at[a:b]),
            (packed, left.at[a:b]),
            (packed.at[0:PAD], right.at[b:b + PAD]),
            (packed.at[0:PAD], left.at[b:b + PAD]),
            (packed.at[high - PAD:high], right.at[0:PAD]),
            (packed.at[high - PAD:high], left.at[0:PAD]),
        ]
        return [
            functools.partial(
                pltpu.make_async_remote_copy, src_ref=src, dst_ref=dst,
                send_sem=send_sem.at[base + d], recv_sem=recv_sem.at[base + d],
                device_id=(around[d][1], around[d][2]), device_id_type=MESH,
            )
            for d, (src, dst) in enumerate(whole)
        ]

    coarse_copies = copies(ce, pc, cl, cr, th, 0)
    fine_copies = copies(fe, pf, fl, fr, fh, 8)

    def start(made):
        for d in (2, 3, 0, 1, 4, 5, 6, 7):
            @pl.when(around[d][0])
            def _(d=d):
                made[d]().start()

    def wait_in(made):
        for d in range(8):
            @pl.when(arrives[d])
            def _(d=d):
                made[d]().wait_recv()

    def wait_out(made):
        for d in range(8):
            @pl.when(around[d][0])
            def _(d=d):
                made[d]().wait_send()

    def blank(ext, left, right, high):
        a, b = PAD, PAD + high
        fields = ext.shape[0]

        @pl.when(jnp.logical_not(up))
        def _():
            ext[:, 0:a, 0:tw] = jnp.zeros((fields, PAD, tw), jnp.float32)
            left[0:a, :] = jnp.zeros((PAD, LANES), jnp.float32)
            right[0:a, :] = jnp.zeros((PAD, LANES), jnp.float32)

        @pl.when(jnp.logical_not(dn))
        def _():
            ext[:, b:b + PAD, 0:tw] = jnp.zeros((fields, PAD, tw), jnp.float32)
            left[b:b + PAD, :] = jnp.zeros((PAD, LANES), jnp.float32)
            right[b:b + PAD, :] = jnp.zeros((PAD, LANES), jnp.float32)

        @pl.when(jnp.logical_not(lf))
        def _():
            left[...] = jnp.zeros(left.shape, jnp.float32)

        @pl.when(jnp.logical_not(rt))
        def _():
            right[...] = jnp.zeros(right.shape, jnp.float32)

    def pack(fields, reach):
        high = fields[0].shape[0]
        lane = lax.broadcasted_iota(jnp.int32, (high, LANES), 1)
        out = None
        for q, field in enumerate(fields):
            edge = jnp.where(lane < LANES // 2, field[:, 0:LANES], field[:, tw - LANES:tw])
            if q == 0:
                out = edge
            else:
                lo = 2 * reach * q - reach
                out = jnp.where((lane >= lo) & (lane < lo + 2 * reach), turn(edge, 2 * reach * q, 1), out)
        return out

    def unpack(ext, left, right, reach):
        lane = lax.broadcasted_iota(jnp.int32, left.shape, 1)
        of_right = lane < reach
        for q in range(1, ext.shape[0]):
            of_right = of_right | ((lane >= 2 * reach * q) & (lane < 2 * reach * q + reach))
        merged = jnp.where(of_right, right[...], left[...])
        for q in range(ext.shape[0]):
            ext[q, :, tw:tw + LANES] = merged if q == 0 else turn(merged, -2 * reach * q, 1)

    eta, depth = eta_ref[...], depth_ref[...]
    f0, f1 = flux_ref[0], flux_ref[1]
    for q, field in enumerate((eta, depth, f0, f1)):
        ce[q, PAD:PAD + th, 0:tw] = field
    pc[...] = pack((eta, depth, f0, f1), 2)
    blank(ce, cl, cr, th)
    pl.semaphore_wait(barrier, expected)
    start(coarse_copies)

    kind = class_ref[...]
    rough = jnp.zeros(kind.shape, jnp.float32)
    for i in range(NCLASS):
        rough = jnp.where(kind == i, manning_ref[i], rough)
    water = wet_ref[...].astype(jnp.float32) * fdepth_ref[...]
    bed = bed_ref[...]
    for q, field in enumerate((water, bed, rough)):
        fe[q, PAD:PAD + fh, 0:tw] = field
    pf[...] = pack((water, bed, rough), FSTEPS)
    blank(fe, fl, fr, fh)
    start(fine_copies)

    wait_in(coarse_copies)
    unpack(ce, cl, cr, 2)
    s, d, fa, fb = ce[0], ce[1], ce[2], ce[3]
    s, fa, fb = coarse_step(s, d, fa, fb)
    cs[0] = s[PAD:PAD + th, 0:tw]
    cs[1] = fa[PAD:PAD + th, 0:tw]
    s, fa, fb = coarse_step(s, d, fa, fb)
    cs[2] = s[PAD:PAD + th, 0:tw]
    cs[3] = fa[PAD:PAD + th, 0:tw]
    out_eta[...] = s[PAD:PAD + th, 0:tw]

    low = (jnp.maximum(c * tw - (tw + REACH) + RATIO - 1, 0)) // RATIO
    seg0 = low + lax.rem(r + nrow - lax.rem(low, nrow), nrow)
    lane_t = lax.broadcasted_iota(jnp.int32, (8, tw), 1)
    values = []
    for slot in range(nslots):
        seg = seg0 + slot * nrow
        cell = nest_ref[jnp.minimum(seg * RATIO, nb - 1)]
        row = cell // width
        col = cell - row * width - c * tw
        row = row - r * th
        held = (row >= 0) & (row < th)
        row = jnp.clip(row, 0, th - 1)
        col = jnp.where(held, col, -1)
        o = slot * 8
        samp[o:o + 1, :] = ce[0, pl.ds(PAD + row, 1), 0:tw]
        samp[o + 1:o + 2, :] = cs[0, pl.ds(row, 1), :]
        samp[o + 2:o + 3, :] = cs[2, pl.ds(row, 1), :]
        samp[o + 3:o + 4, :] = ce[2, pl.ds(PAD + row, 1), 0:tw]
        samp[o + 4:o + 5, :] = cs[1, pl.ds(row, 1), :]
        samp[o + 5:o + 6, :] = cs[3, pl.ds(row, 1), :]
        samp[o + 6:o + 7, :] = ce[1, pl.ds(PAD + row, 1), 0:tw]
        samp[o + 7:o + 8, :] = jnp.zeros((1, tw), jnp.float32)
        got = jnp.where(lane_t == col, samp[o:o + 8, :], 0.0)
        values.append(jnp.sum(got, axis=1, keepdims=True))
    ext_w = tw + LANES
    lane_e = lax.broadcasted_iota(jnp.int32, (8, ext_w), 1)
    place = jnp.where(lane_e < tw + LANES // 2, lane_e, lane_e - ext_w)

    def sample_copy(k):
        return pltpu.make_async_remote_copy(
            src_ref=sbuf.at[k], dst_ref=rbuf.at[k * nrow + r],
            send_sem=ssend_sem.at[k], recv_sem=srecv_sem.at[k * nrow + r],
            device_id=(0, c - k), device_id_type=MESH,
        )

    for k in range(3):
        at = place + (c - k) * tw
        window = jnp.zeros((8, ext_w), jnp.float32)
        for slot in range(nslots):
            begin = (seg0 + slot * nrow) * RATIO
            window = jnp.where((at >= begin) & (at < begin + RATIO), values[slot], window)
        sbuf[k] = window
        sends = (r > 0) if k == 0 else (c - k >= 0)

        @pl.when(sends)
        def _(k=k):
            sample_copy(k).start()

    wait_in(fine_copies)
    unpack(fe, fl, fr, FSTEPS)

    def keeps(high, first):
        row = lax.broadcasted_iota(jnp.int32, (high, ext_w), 0) + first
        lane = lax.broadcasted_iota(jnp.int32, (high, ext_w), 1)
        col = jnp.where(lane < tw + LANES // 2, lane, lane - ext_w) + c * tw
        return row != fh * nrow - 1, (col != -1) & (col != width - 1)

    row_keep, col_keep = keeps(fh + 2 * PAD, r * fh - PAD)
    w, g0, g1 = fine_run(fe[0], fe[1], fe[2], row_keep, col_keep, None)
    out_water[...] = w[PAD:PAD + fh, 0:tw]
    out_flux[0] = g0[PAD:PAD + fh, 0:tw]
    out_flux[1] = g1[PAD:PAD + fh, 0:tw]

    @pl.when(r == 0)
    def _():
        acc[...] = sbuf[0]
        for k in range(3):
            for rr in range(nrow):
                if k == 0 and rr == 0:
                    continue

                @pl.when(c + k < ncol)
                def _(k=k, rr=rr):
                    j = k * nrow + rr
                    pltpu.make_async_remote_copy(
                        src_ref=sbuf.at[k], dst_ref=rbuf.at[j],
                        send_sem=ssend_sem.at[k], recv_sem=srecv_sem.at[j],
                        device_id=(rr, c + k), device_id_type=MESH,
                    ).wait_recv()
                    acc[...] += rbuf[j]
        level_s = [acc[i:i + 1, :] for i in range(3)]
        still = acc[6:7, :]
        level_v = []
        for i in range(3):
            total = still + level_s[i]
            level_v.append(acc[3 + i:4 + i, :] / jnp.where(total == 0.0, 1.0, total))

        def top(step, w0, b0):
            k = step // SUB
            weight = (step % SUB + 1) / SUB
            bs = (1.0 - weight) * level_s[k] + weight * level_s[k + 1]
            bv = (1.0 - weight) * level_v[k] + weight * level_v[k + 1]
            return w0 * bv + jnp.sqrt(gravity * jnp.maximum(w0, depth_floor)) * (bs - (b0 + w0))

        strip = 2 * PAD
        _, ck = keeps(strip, 0)
        w, g0, g1 = fine_run(
            fe[0, PAD:PAD + strip, :], fe[1, PAD:PAD + strip, :], fe[2, PAD:PAD + strip, :],
            None, ck, top,
        )
        out_water[0:PAD, :] = w[0:PAD, 0:tw]
        out_flux[0, 0:PAD, :] = g0[0:PAD, 0:tw]
        out_flux[1, 0:PAD, :] = g1[0:PAD, 0:tw]

    wait_out(coarse_copies)
    wait_out(fine_copies)
    for k in range(3):
        sends = (r > 0) if k == 0 else (c - k >= 0)

        @pl.when(sends)
        def _(k=k):
            sample_copy(k).wait_send()


def per_device(nrow, ncol, *args):
    c_eta, c_flux, c_depth, f_bed, f_depth, f_wet, f_class, manning, nest_map = args
    th, tw = c_eta.shape
    fh = f_bed.shape[0]
    ext_w = tw + LANES
    segments = -(-nest_map.shape[0] // RATIO)
    last_low = max((ncol - 1) * tw - (tw + REACH) + RATIO - 1, 0) // RATIO
    span = max((tw + REACH) // RATIO + 1, segments - last_low)
    nslots = -(-span // nrow)
    vmem = pl.BlockSpec(memory_space=pltpu.VMEM)
    smem = pl.BlockSpec(memory_space=pltpu.SMEM)
    f32 = jnp.float32
    return pl.pallas_call(
        functools.partial(kernel, nrow, ncol, nslots),
        out_shape=(
            jax.ShapeDtypeStruct((th, tw), f32),
            jax.ShapeDtypeStruct((fh, tw), f32),
            jax.ShapeDtypeStruct((2, fh, tw), f32),
        ),
        in_specs=[vmem] * 7 + [smem] * 2,
        out_specs=(vmem, vmem, vmem),
        scratch_shapes=[
            pltpu.VMEM((4, th + 2 * PAD, ext_w), f32),
            pltpu.VMEM((4, th, tw), f32),
            pltpu.VMEM((th, LANES), f32),
            pltpu.VMEM((th + 2 * PAD, LANES), f32),
            pltpu.VMEM((th + 2 * PAD, LANES), f32),
            pltpu.VMEM((3, fh + 2 * PAD, ext_w), f32),
            pltpu.VMEM((fh, LANES), f32),
            pltpu.VMEM((fh + 2 * PAD, LANES), f32),
            pltpu.VMEM((fh + 2 * PAD, LANES), f32),
            pltpu.VMEM((nslots * 8, tw), f32),
            pltpu.VMEM((3, 8, ext_w), f32),
            pltpu.VMEM((3 * nrow, 8, ext_w), f32),
            pltpu.VMEM((8, ext_w), f32),
            pltpu.SemaphoreType.DMA((16,)),
            pltpu.SemaphoreType.DMA((16,)),
            pltpu.SemaphoreType.DMA((3,)),
            pltpu.SemaphoreType.DMA((3 * nrow,)),
        ],
        compiler_params=pltpu.CompilerParams(
            collective_id=0, has_side_effects=True, vmem_limit_bytes=32 * 1024 * 1024
        ),
    )(*args)


def solution(mesh):
    in_specs = (
        P("rows", "cols"),
        P(None, "rows", "cols"),
        P("rows", "cols"),
        P("rows", "cols"),
        P("rows", "cols"),
        P("rows", "cols"),
        P("rows", "cols"),
        P(),
        P(),
    )
    out_specs = (P("rows", "cols"), P("rows", "cols"), P(None, "rows", "cols"))
    body = functools.partial(per_device, mesh.shape["rows"], mesh.shape["cols"])
    return jax.shard_map(body, mesh=mesh, in_specs=in_specs, out_specs=out_specs, check_vma=False)
```

```python
import functools

import jax
import jax.numpy as jnp
from jax import lax
from jax.experimental import pallas as pl
from jax.experimental.pallas import tpu as pltpu
from jax.sharding import PartitionSpec as P

NCLASS = 11
SUB = 3
FSTEPS = 6
RATIO = 18
REACH = 128

gravity = 9.81
coarse_spacing = 90.0
coarse_tick = 0.25
fine_spacing = 5.0
depth_floor = 0.01
dry_depth = 0.05
fine_tick = coarse_tick / SUB

LANES = 128
PAD = 8
MESH = pl.DeviceIdType.MESH


def turn(x, shift, axis):
    return pltpu.roll(x, shift % x.shape[axis], axis)


def coarse_step(surf, depth, rows_flux, cols_flux):
    total = depth + surf

    def face(flux, axis):
        d = jnp.minimum(total, turn(total, -1, axis))
        slope = turn(surf, -1, axis) - surf
        return jnp.minimum(d, 1.0) * (flux - (coarse_tick * gravity / coarse_spacing) * d * slope)

    new_rows = face(rows_flux, 0)
    new_cols = face(cols_flux, 1)
    surf = surf - (coarse_tick / coarse_spacing) * (
        new_rows - turn(new_rows, 1, 0) + (new_cols - turn(new_cols, 1, 1))
    )
    return surf, new_rows, new_cols


def fine_run(water, bed, rough, row_keep, col_keep, top):
    bed_faces = [jnp.maximum(bed, turn(bed, -1, axis)) for axis in (0, 1)]
    drag = []
    for axis in (0, 1):
        n = 0.5 * (rough + turn(rough, -1, axis))
        drag.append((fine_tick * gravity) * n * n)
    keep = (row_keep, col_keep)
    flux = [None, None]
    first_row = lax.broadcasted_iota(jnp.int32, water.shape, 0) == 0
    for step in range(FSTEPS):
        surf = bed + water
        new = []
        for axis in (0, 1):
            after = turn(surf, -1, axis)
            d = jnp.maximum(jnp.maximum(surf, after) - bed_faces[axis], 0.0)
            push = (fine_tick * gravity / fine_spacing) * d * (after - surf)
            wet = jnp.minimum(d * (1.0 / dry_depth), 1.0)
            if step == 0:
                value = wet * (-push)
            else:
                power = jnp.exp((-7.0 / 3.0) * jnp.log(jnp.maximum(d, depth_floor)))
                friction = 1.0 + drag[axis] * jnp.abs(flux[axis]) * power
                value = wet * (flux[axis] - push) / friction
            if keep[axis] is not None:
                value = jnp.where(keep[axis], value, 0.0)
            new.append(value)
        above = turn(new[0], 1, 0)
        if top is not None:
            above = jnp.where(first_row, top(step, water[0:1, :], bed[0:1, :]), above)
        water = water - (fine_tick / fine_spacing) * (new[0] - above + (new[1] - turn(new[1], 1, 1)))
        flux = new
    return water, flux[0], flux[1]


def kernel(
    nrow, ncol, nslots,
    eta_ref, flux_ref, depth_ref, bed_ref, fdepth_ref, wet_ref, class_ref, manning_hbm, nest_hbm,
    out_eta, out_water, out_flux,
    ce, cs, pc, cl, cr, fe, pf, fl, fr, samp, sbuf, rbuf, acc,
    fdepth, wet, kinds, manning, nest,
    send_sem, recv_sem, ssend_sem, srecv_sem, load_sem,
):
    r = lax.axis_index("rows")
    c = lax.axis_index("cols")
    th, tw = eta_ref.shape
    fh = bed_ref.shape[0]
    nb = nest.shape[0]
    width = tw * ncol
    up, dn = r > 0, r < nrow - 1
    lf, rt = c > 0, c < ncol - 1
    around = [
        (up, r - 1, c), (dn, r + 1, c), (lf, r, c - 1), (rt, r, c + 1),
        (up & lf, r - 1, c - 1), (up & rt, r - 1, c + 1),
        (dn & lf, r + 1, c - 1), (dn & rt, r + 1, c + 1),
    ]
    arrives = [dn, up, rt, lf, dn & rt, dn & lf, up & rt, up & lf]

    loads = [
        (eta_ref, ce.at[0, PAD:PAD + th, 0:tw]),
        (depth_ref, ce.at[1, PAD:PAD + th, 0:tw]),
        (flux_ref, ce.at[2:4, PAD:PAD + th, 0:tw]),
        (class_ref, kinds), (manning_hbm, manning), (wet_ref, wet), (fdepth_ref, fdepth),
        (bed_ref, fe.at[1, PAD:PAD + fh, 0:tw]), (nest_hbm, nest),
    ]
    loads = [pltpu.make_async_copy(a, b, load_sem.at[i]) for i, (a, b) in enumerate(loads)]
    barrier = pltpu.get_barrier_semaphore()
    expected = jnp.int32(0)
    for there, rr, cc in around:
        @pl.when(there)
        def _(rr=rr, cc=cc):
            pl.semaphore_signal(barrier, inc=1, device_id=(rr, cc), device_id_type=MESH)
        expected = expected + there.astype(jnp.int32)

    @pl.when(r == 0)
    def _():
        for k in range(3):
            for rr in range(nrow):
                if k == 0 and rr == 0:
                    continue

                @pl.when(c + k < ncol)
                def _(k=k, rr=rr):
                    pl.semaphore_signal(barrier, inc=1, device_id=(rr, c + k), device_id_type=MESH)

    for k in range(3):
        sends = c - k >= 0
        if k == 0:
            sends = r > 0
        expected = expected + sends.astype(jnp.int32)

    for load in loads:
        load.start()

    def copies(ext, packed, left, right, high, base):
        a, b = PAD, PAD + high
        n = packed.shape[0]
        z = PAD + n
        whole = [
            (ext.at[:, a:a + PAD, 0:tw], ext.at[:, b:b + PAD, 0:tw]),
            (ext.at[:, b - PAD:b, 0:tw], ext.at[:, 0:a, 0:tw]),
            (packed, right.at[PAD:z]),
            (packed, left.at[PAD:z]),
            (packed.at[0:PAD], right.at[z:z + PAD]),
            (packed.at[0:PAD], left.at[z:z + PAD]),
            (packed.at[n - PAD:n], right.at[0:PAD]),
            (packed.at[n - PAD:n], left.at[0:PAD]),
        ]
        return [
            functools.partial(
                pltpu.make_async_remote_copy, src_ref=src, dst_ref=dst,
                send_sem=send_sem.at[base + d], recv_sem=recv_sem.at[base + d],
                device_id=(around[d][1], around[d][2]), device_id_type=MESH,
            )
            for d, (src, dst) in enumerate(whole)
        ]

    coarse_copies = copies(ce, pc, cl, cr, th, 0)
    fine_copies = copies(fe, pf, fl, fr, fh, 8)

    def start(made, which):
        for d in which:
            @pl.when(around[d][0])
            def _(d=d):
                made[d]().start()

    def wait_in(made):
        for d in range(8):
            @pl.when(arrives[d])
            def _(d=d):
                made[d]().wait_recv()

    def wait_out(made):
        for d in range(8):
            @pl.when(around[d][0])
            def _(d=d):
                made[d]().wait_send()

    def blank(ext, left, right, high):
        a, b = PAD, PAD + high
        fields = ext.shape[0]
        z = left.shape[0] - PAD

        @pl.when(jnp.logical_not(up))
        def _():
            ext[:, 0:a, 0:tw] = jnp.zeros((fields, PAD, tw), jnp.float32)
            left[0:a, :] = jnp.zeros((PAD, LANES), jnp.float32)
            right[0:a, :] = jnp.zeros((PAD, LANES), jnp.float32)

        @pl.when(jnp.logical_not(dn))
        def _():
            ext[:, b:b + PAD, 0:tw] = jnp.zeros((fields, PAD, tw), jnp.float32)
            left[z:z + PAD, :] = jnp.zeros((PAD, LANES), jnp.float32)
            right[z:z + PAD, :] = jnp.zeros((PAD, LANES), jnp.float32)

        @pl.when(jnp.logical_not(lf))
        def _():
            left[...] = jnp.zeros(left.shape, jnp.float32)

        @pl.when(jnp.logical_not(rt))
        def _():
            right[...] = jnp.zeros(right.shape, jnp.float32)

    def pack(fields, reach, fold):
        high = fields[0].shape[0]
        part = high // fold
        step = 2 * reach * len(fields) if fold > 1 else 0
        lane = lax.broadcasted_iota(jnp.int32, (part, LANES), 1)
        out = None
        for q, field in enumerate(fields):
            edge = jnp.where(
                lax.broadcasted_iota(jnp.int32, (high, LANES), 1) < LANES // 2,
                field[:, 0:LANES], field[:, tw - LANES:tw],
            )
            for g in range(fold):
                shift = g * step + 2 * reach * q
                piece = edge[g * part:(g + 1) * part]
                if shift == 0:
                    out = piece
                else:
                    lo = shift - reach
                    out = jnp.where((lane >= lo) & (lane < lo + 2 * reach), turn(piece, shift, 1), out)
        return out

    def unpack(ext, left, right, reach, fold):
        lane = lax.broadcasted_iota(jnp.int32, left.shape, 1)
        fields = ext.shape[0]
        step = 2 * reach * fields if fold > 1 else 0
        of_right = lane < reach
        for i in range(1, fields * fold):
            of_right = of_right | ((lane >= 2 * reach * i) & (lane < 2 * reach * i + reach))
        merged = jnp.where(of_right, right[...], left[...])
        part = left.shape[0] - 2 * PAD
        for q in range(fields):
            pieces = [(0, PAD, fold - 1, 0), (PAD + part, part + 2 * PAD, 0, PAD + fold * part)]
            pieces += [(PAD, PAD + part, g, PAD + g * part) for g in range(fold)]
            for lo, hi, g, at in pieces:
                shift = g * step + 2 * reach * q
                piece = merged[lo:hi]
                if shift:
                    piece = turn(piece, -shift, 1)
                ext[q, at:at + hi - lo, tw:tw + LANES] = piece

    fold = th // 16
    blank(ce, cl, cr, th)
    for load in loads[:3]:
        load.wait()
    pl.semaphore_wait(barrier, expected)
    start(coarse_copies, (0, 1))
    pc[...] = pack([ce[q, PAD:PAD + th, 0:tw] for q in range(4)], 2, fold)
    start(coarse_copies, (2, 3, 4, 5, 6, 7))

    for load in loads[3:]:
        load.wait()
    kind = kinds[...]
    rough = jnp.zeros(kind.shape, jnp.float32)
    for i in range(NCLASS):
        rough = jnp.where(kind == i, manning[i], rough)
    water = wet[...].astype(jnp.float32) * fdepth[...]
    bed = fe[1, PAD:PAD + fh, 0:tw]
    fe[0, PAD:PAD + fh, 0:tw] = water
    fe[2, PAD:PAD + fh, 0:tw] = rough
    pf[...] = pack((water, bed, rough), FSTEPS, 1)
    blank(fe, fl, fr, fh)
    start(fine_copies, (0, 1, 2, 3, 4, 5, 6, 7))

    wait_in(coarse_copies)
    unpack(ce, cl, cr, 2, fold)
    s, d, fa, fb = ce[0], ce[1], ce[2], ce[3]
    s, fa, fb = coarse_step(s, d, fa, fb)
    cs[0] = s[PAD:PAD + th, 0:tw]
    cs[1] = fa[PAD:PAD + th, 0:tw]
    s, fa, fb = coarse_step(s, d, fa, fb)
    cs[2] = s[PAD:PAD + th, 0:tw]
    cs[3] = fa[PAD:PAD + th, 0:tw]
    out_eta[...] = s[PAD:PAD + th, 0:tw]

    low = (jnp.maximum(c * tw - (tw + REACH) + RATIO - 1, 0)) // RATIO
    seg0 = low + lax.rem(r + nrow - lax.rem(low, nrow), nrow)
    lane_t = lax.broadcasted_iota(jnp.int32, (8, tw), 1)
    values = []
    for slot in range(nslots):
        seg = seg0 + slot * nrow
        cell = nest[jnp.minimum(seg * RATIO, nb - 1)]
        row = cell // width
        col = cell - row * width - c * tw
        row = row - r * th
        held = (row >= 0) & (row < th)
        row = jnp.clip(row, 0, th - 1)
        col = jnp.where(held, col, -1)
        o = slot * 8
        samp[o:o + 1, :] = ce[0, pl.ds(PAD + row, 1), 0:tw]
        samp[o + 1:o + 2, :] = cs[0, pl.ds(row, 1), :]
        samp[o + 2:o + 3, :] = cs[2, pl.ds(row, 1), :]
        samp[o + 3:o + 4, :] = ce[2, pl.ds(PAD + row, 1), 0:tw]
        samp[o + 4:o + 5, :] = cs[1, pl.ds(row, 1), :]
        samp[o + 5:o + 6, :] = cs[3, pl.ds(row, 1), :]
        samp[o + 6:o + 7, :] = ce[1, pl.ds(PAD + row, 1), 0:tw]
        samp[o + 7:o + 8, :] = jnp.zeros((1, tw), jnp.float32)
        got = jnp.where(lane_t == col, samp[o:o + 8, :], 0.0)
        values.append(jnp.sum(got, axis=1, keepdims=True))
    ext_w = tw + LANES
    lane_e = lax.broadcasted_iota(jnp.int32, (8, ext_w), 1)
    place = jnp.where(lane_e < tw + LANES // 2, lane_e, lane_e - ext_w)

    def sample_copy(k):
        return pltpu.make_async_remote_copy(
            src_ref=sbuf.at[k], dst_ref=rbuf.at[k * nrow + r],
            send_sem=ssend_sem.at[k], recv_sem=srecv_sem.at[k * nrow + r],
            device_id=(0, c - k), device_id_type=MESH,
        )

    def window_start(cc):
        return jnp.maximum(cc * tw - FSTEPS, 0) // RATIO

    lane_s = lax.broadcasted_iota(jnp.int32, (8, LANES), 1)
    for k in range(3):
        at = lane_s + window_start(c - k)
        window = jnp.zeros((8, LANES), jnp.float32)
        for slot in range(nslots):
            window = jnp.where(at == seg0 + slot * nrow, values[slot], window)
        sbuf[k] = window
        sends = (r > 0) if k == 0 else (c - k >= 0)

        @pl.when(sends)
        def _(k=k):
            sample_copy(k).start()

    wait_in(fine_copies)
    unpack(fe, fl, fr, FSTEPS, 1)

    def keeps(high, first):
        row = lax.broadcasted_iota(jnp.int32, (high, ext_w), 0) + first
        lane = lax.broadcasted_iota(jnp.int32, (high, ext_w), 1)
        col = jnp.where(lane < tw + LANES // 2, lane, lane - ext_w) + c * tw
        return row != fh * nrow - 1, (col != -1) & (col != width - 1)

    row_keep, col_keep = keeps(fh + 2 * PAD, r * fh - PAD)
    w, g0, g1 = fine_run(fe[0], fe[1], fe[2], row_keep, col_keep, None)
    out_water[...] = w[PAD:PAD + fh, 0:tw]
    out_flux[0] = g0[PAD:PAD + fh, 0:tw]
    out_flux[1] = g1[PAD:PAD + fh, 0:tw]

    @pl.when(r == 0)
    def _():
        total = sbuf[0]
        for k in range(3):
            for rr in range(nrow):
                if k == 0 and rr == 0:
                    continue

                @pl.when(c + k < ncol)
                def _(k=k, rr=rr):
                    j = k * nrow + rr
                    pltpu.make_async_remote_copy(
                        src_ref=sbuf.at[k], dst_ref=rbuf.at[j],
                        send_sem=ssend_sem.at[k], recv_sem=srecv_sem.at[j],
                        device_id=(rr, c + k), device_id_type=MESH,
                    ).wait_recv()
        for k in range(3):
            for rr in range(nrow):
                if k == 0 and rr == 0:
                    continue
                total = total + jnp.where(c + k < ncol, rbuf[k * nrow + rr], 0.0)
        first = window_start(c)
        at = place + c * tw
        spread = jnp.zeros((8, ext_w), jnp.float32)
        for i in range((tw + 2 * FSTEPS) // RATIO + 2):
            begin = (first + i) * RATIO
            spread = jnp.where((at >= begin) & (at < begin + RATIO), total[:, i:i + 1], spread)
        acc[...] = spread
        level_s = [acc[i:i + 1, :] for i in range(3)]
        still = acc[6:7, :]
        level_v = []
        for i in range(3):
            total = still + level_s[i]
            level_v.append(acc[3 + i:4 + i, :] / jnp.where(total == 0.0, 1.0, total))

        def top(step, w0, b0):
            k = step // SUB
            weight = (step % SUB + 1) / SUB
            bs = (1.0 - weight) * level_s[k] + weight * level_s[k + 1]
            bv = (1.0 - weight) * level_v[k] + weight * level_v[k + 1]
            return w0 * bv + jnp.sqrt(gravity * jnp.maximum(w0, depth_floor)) * (bs - (b0 + w0))

        strip = 2 * PAD
        _, ck = keeps(strip, 0)
        w, g0, g1 = fine_run(
            fe[0, PAD:PAD + strip, :], fe[1, PAD:PAD + strip, :], fe[2, PAD:PAD + strip, :],
            None, ck, top,
        )
        out_water[0:PAD, :] = w[0:PAD, 0:tw]
        out_flux[0, 0:PAD, :] = g0[0:PAD, 0:tw]
        out_flux[1, 0:PAD, :] = g1[0:PAD, 0:tw]

    wait_out(coarse_copies)
    wait_out(fine_copies)
    for k in range(3):
        sends = (r > 0) if k == 0 else (c - k >= 0)

        @pl.when(sends)
        def _(k=k):
            sample_copy(k).wait_send()


def deliver(a, b, c, to_a, to_b, to_c, sem):
    moves = [
        pltpu.make_async_copy(src, dst, sem.at[i])
        for i, (src, dst) in enumerate(((a, to_a), (b, to_b), (c, to_c)))
    ]
    for move in moves:
        move.start()
    for move in moves:
        move.wait()


def per_device(nrow, ncol, *args):
    c_eta, c_flux, c_depth, f_bed, f_depth, f_wet, f_class, manning, nest_map = args
    th, tw = c_eta.shape
    fh = f_bed.shape[0]
    ext_w = tw + LANES
    segments = -(-nest_map.shape[0] // RATIO)
    last_low = max((ncol - 1) * tw - (tw + REACH) + RATIO - 1, 0) // RATIO
    span = max((tw + REACH) // RATIO + 1, segments - last_low)
    nslots = -(-span // nrow)
    vmem = pl.BlockSpec(memory_space=pltpu.VMEM)
    hbm = pl.BlockSpec(memory_space=pltpu.HBM)
    f32 = jnp.float32
    shapes = (
        jax.ShapeDtypeStruct((th, tw), f32),
        jax.ShapeDtypeStruct((fh, tw), f32),
        jax.ShapeDtypeStruct((2, fh, tw), f32),
    )
    outs = pl.pallas_call(
        functools.partial(kernel, nrow, ncol, nslots),
        out_shape=shapes,
        in_specs=[hbm] * 9,
        out_specs=(vmem, vmem, vmem),
        scratch_shapes=[
            pltpu.VMEM((4, th + 2 * PAD, ext_w), f32),
            pltpu.VMEM((4, th, tw), f32),
            pltpu.VMEM((16, LANES), f32),
            pltpu.VMEM((16 + 2 * PAD, LANES), f32),
            pltpu.VMEM((16 + 2 * PAD, LANES), f32),
            pltpu.VMEM((3, fh + 2 * PAD, ext_w), f32),
            pltpu.VMEM((fh, LANES), f32),
            pltpu.VMEM((fh + 2 * PAD, LANES), f32),
            pltpu.VMEM((fh + 2 * PAD, LANES), f32),
            pltpu.VMEM((nslots * 8, tw), f32),
            pltpu.VMEM((3, 8, LANES), f32),
            pltpu.VMEM((3 * nrow, 8, LANES), f32),
            pltpu.VMEM((8, ext_w), f32),
            pltpu.VMEM((fh, tw), f32),
            pltpu.VMEM((fh, tw), jnp.int32),
            pltpu.VMEM((fh, tw), jnp.int32),
            pltpu.SMEM(manning.shape, f32),
            pltpu.SMEM(nest_map.shape, jnp.int32),
            pltpu.SemaphoreType.DMA((16,)),
            pltpu.SemaphoreType.DMA((16,)),
            pltpu.SemaphoreType.DMA((3,)),
            pltpu.SemaphoreType.DMA((3 * nrow,)),
            pltpu.SemaphoreType.DMA((9,)),
        ],
        compiler_params=pltpu.CompilerParams(
            collective_id=0, has_side_effects=True, vmem_limit_bytes=60 * 1024 * 1024
        ),
    )(*args)
    return pl.pallas_call(
        deliver,
        out_shape=shapes,
        in_specs=[hbm] * 3,
        out_specs=(hbm, hbm, hbm),
        scratch_shapes=[pltpu.SemaphoreType.DMA((3,))],
    )(*outs)


def solution(mesh):
    in_specs = (
        P("rows", "cols"),
        P(None, "rows", "cols"),
        P("rows", "cols"),
        P("rows", "cols"),
        P("rows", "cols"),
        P("rows", "cols"),
        P("rows", "cols"),
        P(),
        P(),
    )
    out_specs = (P("rows", "cols"), P("rows", "cols"), P(None, "rows", "cols"))
    body = functools.partial(per_device, mesh.shape["rows"], mesh.shape["cols"])
    return jax.shard_map(body, mesh=mesh, in_specs=in_specs, out_specs=out_specs, check_vma=False)
```

```python
import functools

import jax
import jax.numpy as jnp
from jax import lax
from jax.experimental import pallas as pl
from jax.experimental.pallas import tpu as pltpu
from jax.sharding import PartitionSpec as P

NCLASS = 11
SUB = 3
FSTEPS = 6
RATIO = 18
REACH = 128

gravity = 9.81
coarse_spacing = 90.0
coarse_tick = 0.25
fine_spacing = 5.0
depth_floor = 0.01
dry_depth = 0.05
fine_tick = coarse_tick / SUB

LANES = 128
PAD = 8
MESH = pl.DeviceIdType.MESH


def turn(x, shift, axis):
    return pltpu.roll(x, shift % x.shape[axis], axis)


def coarse_step(surf, depth, rows_flux, cols_flux):
    total = depth + surf

    def face(flux, axis):
        d = jnp.minimum(total, turn(total, -1, axis))
        slope = turn(surf, -1, axis) - surf
        return jnp.minimum(d, 1.0) * (flux - (coarse_tick * gravity / coarse_spacing) * d * slope)

    new_rows = face(rows_flux, 0)
    new_cols = face(cols_flux, 1)
    surf = surf - (coarse_tick / coarse_spacing) * (
        new_rows - turn(new_rows, 1, 0) + (new_cols - turn(new_cols, 1, 1))
    )
    return surf, new_rows, new_cols


def fine_run(water, bed, rough, row_keep, col_keep, top, steps=FSTEPS):
    bed_faces = [jnp.maximum(bed, turn(bed, -1, axis)) for axis in (0, 1)]
    drag = []
    for axis in (0, 1):
        n = 0.5 * (rough + turn(rough, -1, axis))
        drag.append((fine_tick * gravity) * n * n)
    keep = (row_keep, col_keep)
    flux = [None, None]
    first_row = lax.broadcasted_iota(jnp.int32, water.shape, 0) == 0
    for step in range(steps):
        surf = bed + water
        new = []
        for axis in (0, 1):
            after = turn(surf, -1, axis)
            d = jnp.maximum(jnp.maximum(surf, after) - bed_faces[axis], 0.0)
            push = (fine_tick * gravity / fine_spacing) * d * (after - surf)
            wet = jnp.minimum(d * (1.0 / dry_depth), 1.0)
            if step == 0:
                value = wet * (-push)
            else:
                power = jnp.exp((-7.0 / 3.0) * jnp.log(jnp.maximum(d, depth_floor)))
                friction = 1.0 + drag[axis] * jnp.abs(flux[axis]) * power
                value = wet * (flux[axis] - push) / friction
            if keep[axis] is not None:
                value = jnp.where(keep[axis], value, 0.0)
            new.append(value)
        above = turn(new[0], 1, 0)
        if top is not None:
            above = jnp.where(first_row, top(step, water[0:1, :], bed[0:1, :]), above)
        water = water - (fine_tick / fine_spacing) * (new[0] - above + (new[1] - turn(new[1], 1, 1)))
        flux = new
    return water, flux[0], flux[1]


def kernel(
    nrow, ncol, nslots,
    eta_ref, flux_ref, depth_ref, bed_ref, fdepth_ref, wet_ref, class_ref, manning_hbm, nest_hbm,
    out_eta, out_water, out_flux,
    ce, cs, pc, cl, cr, fe, pf, fl, fr, samp, sbuf, rbuf, acc,
    fdepth, wet, kinds, manning, nest,
    send_sem, recv_sem, ssend_sem, srecv_sem, load_sem,
):
    r = lax.axis_index("rows")
    c = lax.axis_index("cols")
    th, tw = eta_ref.shape
    fh = bed_ref.shape[0]
    nb = nest.shape[0]
    width = tw * ncol
    up, dn = r > 0, r < nrow - 1
    lf, rt = c > 0, c < ncol - 1
    around = [
        (up, r - 1, c), (dn, r + 1, c), (lf, r, c - 1), (rt, r, c + 1),
        (up & lf, r - 1, c - 1), (up & rt, r - 1, c + 1),
        (dn & lf, r + 1, c - 1), (dn & rt, r + 1, c + 1),
    ]
    arrives = [dn, up, rt, lf, dn & rt, dn & lf, up & rt, up & lf]

    loads = [
        (eta_ref, ce.at[0, PAD:PAD + th, 0:tw]),
        (depth_ref, ce.at[1, PAD:PAD + th, 0:tw]),
        (flux_ref, ce.at[2:4, PAD:PAD + th, 0:tw]),
        (class_ref, kinds), (manning_hbm, manning), (wet_ref, wet), (fdepth_ref, fdepth),
        (bed_ref, fe.at[1, PAD:PAD + fh, 0:tw]), (nest_hbm, nest),
    ]
    loads = [pltpu.make_async_copy(a, b, load_sem.at[i]) for i, (a, b) in enumerate(loads)]
    barrier = pltpu.get_barrier_semaphore()
    expected = jnp.int32(0)
    for there, rr, cc in around:
        @pl.when(there)
        def _(rr=rr, cc=cc):
            pl.semaphore_signal(barrier, inc=1, device_id=(rr, cc), device_id_type=MESH)
        expected = expected + there.astype(jnp.int32)

    @pl.when(r == 0)
    def _():
        for k in range(3):
            for rr in range(nrow):
                if k == 0 and rr == 0:
                    continue

                @pl.when(c + k < ncol)
                def _(k=k, rr=rr):
                    pl.semaphore_signal(barrier, inc=1, device_id=(rr, c + k), device_id_type=MESH)

    for k in range(3):
        sends = c - k >= 0
        if k == 0:
            sends = r > 0
        expected = expected + sends.astype(jnp.int32)

    for load in loads:
        load.start()

    def copies(ext, packed, left, right, high, base):
        a, b = PAD, PAD + high
        n = packed.shape[0]
        z = PAD + n
        whole = [
            (ext.at[:, a:a + PAD, 0:tw], ext.at[:, b:b + PAD, 0:tw]),
            (ext.at[:, b - PAD:b, 0:tw], ext.at[:, 0:a, 0:tw]),
            (packed, right.at[PAD:z]),
            (packed, left.at[PAD:z]),
            (packed.at[0:PAD], right.at[z:z + PAD]),
            (packed.at[0:PAD], left.at[z:z + PAD]),
            (packed.at[n - PAD:n], right.at[0:PAD]),
            (packed.at[n - PAD:n], left.at[0:PAD]),
        ]
        return [
            functools.partial(
                pltpu.make_async_remote_copy, src_ref=src, dst_ref=dst,
                send_sem=send_sem.at[base + d], recv_sem=recv_sem.at[base + d],
                device_id=(around[d][1], around[d][2]), device_id_type=MESH,
            )
            for d, (src, dst) in enumerate(whole)
        ]

    coarse_copies = copies(ce, pc, cl, cr, th, 0)
    fine_copies = copies(fe, pf, fl, fr, fh, 8)

    def start(made, which):
        for d in which:
            @pl.when(around[d][0])
            def _(d=d):
                made[d]().start()

    def wait_in(made):
        for d in range(8):
            @pl.when(arrives[d])
            def _(d=d):
                made[d]().wait_recv()

    def wait_out(made):
        for d in range(8):
            @pl.when(around[d][0])
            def _(d=d):
                made[d]().wait_send()

    def blank(ext, left, right, high):
        a, b = PAD, PAD + high
        fields = ext.shape[0]
        z = left.shape[0] - PAD

        @pl.when(jnp.logical_not(up))
        def _():
            ext[:, 0:a, 0:tw] = jnp.zeros((fields, PAD, tw), jnp.float32)
            left[0:a, :] = jnp.zeros((PAD, LANES), jnp.float32)
            right[0:a, :] = jnp.zeros((PAD, LANES), jnp.float32)

        @pl.when(jnp.logical_not(dn))
        def _():
            ext[:, b:b + PAD, 0:tw] = jnp.zeros((fields, PAD, tw), jnp.float32)
            left[z:z + PAD, :] = jnp.zeros((PAD, LANES), jnp.float32)
            right[z:z + PAD, :] = jnp.zeros((PAD, LANES), jnp.float32)

        @pl.when(jnp.logical_not(lf))
        def _():
            left[...] = jnp.zeros(left.shape, jnp.float32)

        @pl.when(jnp.logical_not(rt))
        def _():
            right[...] = jnp.zeros(right.shape, jnp.float32)

    def pack(fields, reach, fold):
        high = fields[0].shape[0]
        part = high // fold
        step = 2 * reach * len(fields) if fold > 1 else 0
        lane = lax.broadcasted_iota(jnp.int32, (part, LANES), 1)
        out = None
        for q, field in enumerate(fields):
            edge = jnp.where(
                lax.broadcasted_iota(jnp.int32, (high, LANES), 1) < LANES // 2,
                field[:, 0:LANES], field[:, tw - LANES:tw],
            )
            for g in range(fold):
                shift = g * step + 2 * reach * q
                piece = edge[g * part:(g + 1) * part]
                if shift == 0:
                    out = piece
                else:
                    lo = shift - reach
                    out = jnp.where((lane >= lo) & (lane < lo + 2 * reach), turn(piece, shift, 1), out)
        return out

    def unpack(ext, left, right, reach, fold):
        lane = lax.broadcasted_iota(jnp.int32, left.shape, 1)
        fields = ext.shape[0]
        step = 2 * reach * fields if fold > 1 else 0
        of_right = lane < reach
        for i in range(1, fields * fold):
            of_right = of_right | ((lane >= 2 * reach * i) & (lane < 2 * reach * i + reach))
        merged = jnp.where(of_right, right[...], left[...])
        part = left.shape[0] - 2 * PAD
        for q in range(fields):
            pieces = [(0, PAD, fold - 1, 0), (PAD + part, part + 2 * PAD, 0, PAD + fold * part)]
            pieces += [(PAD, PAD + part, g, PAD + g * part) for g in range(fold)]
            for lo, hi, g, at in pieces:
                shift = g * step + 2 * reach * q
                piece = merged[lo:hi]
                if shift:
                    piece = turn(piece, -shift, 1)
                ext[q, at:at + hi - lo, tw:tw + LANES] = piece

    fold = th // 16
    blank(ce, cl, cr, th)
    for load in loads[:3]:
        load.wait()
    pl.semaphore_wait(barrier, expected)
    start(coarse_copies, (0, 1))
    pc[...] = pack([ce[q, PAD:PAD + th, 0:tw] for q in range(4)], 2, fold)
    start(coarse_copies, (2, 3, 4, 5, 6, 7))

    for load in loads[3:]:
        load.wait()
    kind = kinds[...]
    rough = jnp.zeros(kind.shape, jnp.float32)
    for i in range(NCLASS):
        rough = jnp.where(kind == i, manning[i], rough)
    water = wet[...].astype(jnp.float32) * fdepth[...]
    bed = fe[1, PAD:PAD + fh, 0:tw]
    fe[0, PAD:PAD + fh, 0:tw] = water
    fe[2, PAD:PAD + fh, 0:tw] = rough
    pf[...] = pack((water, bed, rough), FSTEPS, 1)
    blank(fe, fl, fr, fh)
    start(fine_copies, (0, 1, 2, 3, 4, 5, 6, 7))

    wait_in(coarse_copies)
    unpack(ce, cl, cr, 2, fold)
    s, d, fa, fb = ce[0], ce[1], ce[2], ce[3]
    s, fa, fb = coarse_step(s, d, fa, fb)
    cs[0] = s[PAD:PAD + th, 0:tw]
    cs[1] = fa[PAD:PAD + th, 0:tw]
    s, fa, fb = coarse_step(s, d, fa, fb)
    cs[2] = s[PAD:PAD + th, 0:tw]
    cs[3] = fa[PAD:PAD + th, 0:tw]
    out_eta[...] = s[PAD:PAD + th, 0:tw]

    low = (jnp.maximum(c * tw - (tw + REACH) + RATIO - 1, 0)) // RATIO
    seg0 = low + lax.rem(r + nrow - lax.rem(low, nrow), nrow)
    lane_t = lax.broadcasted_iota(jnp.int32, (8, tw), 1)
    values = []
    for slot in range(nslots):
        seg = seg0 + slot * nrow
        cell = nest[jnp.minimum(seg * RATIO, nb - 1)]
        row = cell // width
        col = cell - row * width - c * tw
        row = row - r * th
        held = (row >= 0) & (row < th)
        row = jnp.clip(row, 0, th - 1)
        col = jnp.where(held, col, -1)
        o = slot * 8
        samp[o:o + 1, :] = ce[0, pl.ds(PAD + row, 1), 0:tw]
        samp[o + 1:o + 2, :] = cs[0, pl.ds(row, 1), :]
        samp[o + 2:o + 3, :] = cs[2, pl.ds(row, 1), :]
        samp[o + 3:o + 4, :] = ce[2, pl.ds(PAD + row, 1), 0:tw]
        samp[o + 4:o + 5, :] = cs[1, pl.ds(row, 1), :]
        samp[o + 5:o + 6, :] = cs[3, pl.ds(row, 1), :]
        samp[o + 6:o + 7, :] = ce[1, pl.ds(PAD + row, 1), 0:tw]
        samp[o + 7:o + 8, :] = jnp.zeros((1, tw), jnp.float32)
        got = jnp.where(lane_t == col, samp[o:o + 8, :], 0.0)
        values.append(jnp.sum(got, axis=1, keepdims=True))
    ext_w = tw + LANES
    lane_e = lax.broadcasted_iota(jnp.int32, (8, ext_w), 1)
    place = jnp.where(lane_e < tw + LANES // 2, lane_e, lane_e - ext_w)

    def sample_copy(k):
        return pltpu.make_async_remote_copy(
            src_ref=sbuf.at[k], dst_ref=rbuf.at[k * nrow + r],
            send_sem=ssend_sem.at[k], recv_sem=srecv_sem.at[k * nrow + r],
            device_id=(0, c - k), device_id_type=MESH,
        )

    def window_start(cc):
        return jnp.maximum(cc * tw - FSTEPS, 0) // RATIO

    lane_s = lax.broadcasted_iota(jnp.int32, (8, LANES), 1)
    for k in range(3):
        at = lane_s + window_start(c - k)
        window = jnp.zeros((8, LANES), jnp.float32)
        for slot in range(nslots):
            window = jnp.where(at == seg0 + slot * nrow, values[slot], window)
        sbuf[k] = window
        sends = (r > 0) if k == 0 else (c - k >= 0)

        @pl.when(sends)
        def _(k=k):
            sample_copy(k).start()

    wait_in(fine_copies)
    unpack(fe, fl, fr, FSTEPS, 1)

    def keeps(high, first):
        row = lax.broadcasted_iota(jnp.int32, (high, ext_w), 0) + first
        lane = lax.broadcasted_iota(jnp.int32, (high, ext_w), 1)
        col = jnp.where(lane < tw + LANES // 2, lane, lane - ext_w) + c * tw
        return row != fh * nrow - 1, (col != -1) & (col != width - 1)

    row_keep, col_keep = keeps(fh + 2 * PAD, r * fh - PAD)
    w, g0, g1 = fine_run(fe[0], fe[1], fe[2], row_keep, col_keep, None)
    out_water[...] = w[PAD:PAD + fh, 0:tw]
    out_flux[0] = g0[PAD:PAD + fh, 0:tw]
    out_flux[1] = g1[PAD:PAD + fh, 0:tw]

    @pl.when(r == 0)
    def _():
        total = sbuf[0]
        for k in range(3):
            for rr in range(nrow):
                if k == 0 and rr == 0:
                    continue

                @pl.when(c + k < ncol)
                def _(k=k, rr=rr):
                    j = k * nrow + rr
                    pltpu.make_async_remote_copy(
                        src_ref=sbuf.at[k], dst_ref=rbuf.at[j],
                        send_sem=ssend_sem.at[k], recv_sem=srecv_sem.at[j],
                        device_id=(rr, c + k), device_id_type=MESH,
                    ).wait_recv()
        for k in range(3):
            for rr in range(nrow):
                if k == 0 and rr == 0:
                    continue
                total = total + jnp.where(c + k < ncol, rbuf[k * nrow + rr], 0.0)
        first = window_start(c)
        at = place + c * tw
        spread = jnp.zeros((8, ext_w), jnp.float32)
        for i in range((tw + 2 * FSTEPS) // RATIO + 2):
            begin = (first + i) * RATIO
            spread = jnp.where((at >= begin) & (at < begin + RATIO), total[:, i:i + 1], spread)
        acc[...] = spread
        level_s = [acc[i:i + 1, :] for i in range(3)]
        still = acc[6:7, :]
        level_v = []
        for i in range(3):
            total = still + level_s[i]
            level_v.append(acc[3 + i:4 + i, :] / jnp.where(total == 0.0, 1.0, total))

        def top(step, w0, b0):
            k = step // SUB
            weight = (step % SUB + 1) / SUB
            bs = (1.0 - weight) * level_s[k] + weight * level_s[k + 1]
            bv = (1.0 - weight) * level_v[k] + weight * level_v[k + 1]
            return w0 * bv + jnp.sqrt(gravity * jnp.maximum(w0, depth_floor)) * (bs - (b0 + w0))

        strip = 2 * PAD
        _, ck = keeps(strip, 0)
        w, g0, g1 = fine_run(
            fe[0, PAD:PAD + strip, :], fe[1, PAD:PAD + strip, :], fe[2, PAD:PAD + strip, :],
            None, ck, top,
        )
        out_water[0:PAD, :] = w[0:PAD, 0:tw]
        out_flux[0, 0:PAD, :] = g0[0:PAD, 0:tw]
        out_flux[1, 0:PAD, :] = g1[0:PAD, 0:tw]

    wait_out(coarse_copies)
    wait_out(fine_copies)
    for k in range(3):
        sends = (r > 0) if k == 0 else (c - k >= 0)

        @pl.when(sends)
        def _(k=k):
            sample_copy(k).wait_send()


def deliver(a, b, c, to_a, to_b, to_c, sem):
    moves = [
        pltpu.make_async_copy(src, dst, sem.at[i])
        for i, (src, dst) in enumerate(((a, to_a), (b, to_b), (c, to_c)))
    ]
    for move in moves:
        move.start()
    for move in moves:
        move.wait()


def per_device(nrow, ncol, *args):
    c_eta, c_flux, c_depth, f_bed, f_depth, f_wet, f_class, manning, nest_map = args
    th, tw = c_eta.shape
    fh = f_bed.shape[0]
    ext_w = tw + LANES
    segments = -(-nest_map.shape[0] // RATIO)
    last_low = max((ncol - 1) * tw - (tw + REACH) + RATIO - 1, 0) // RATIO
    span = max((tw + REACH) // RATIO + 1, segments - last_low)
    nslots = -(-span // nrow)
    vmem = pl.BlockSpec(memory_space=pltpu.VMEM)
    hbm = pl.BlockSpec(memory_space=pltpu.HBM)
    f32 = jnp.float32
    shapes = (
        jax.ShapeDtypeStruct((th, tw), f32),
        jax.ShapeDtypeStruct((fh, tw), f32),
        jax.ShapeDtypeStruct((2, fh, tw), f32),
    )
    outs = pl.pallas_call(
        functools.partial(kernel, nrow, ncol, nslots),
        out_shape=tuple(pltpu.VMEM(x.shape, f32) for x in shapes),
        in_specs=[hbm] * 9,
        out_specs=(vmem, vmem, vmem),
        scratch_shapes=[
            pltpu.VMEM((4, th + 2 * PAD, ext_w), f32),
            pltpu.VMEM((4, th, tw), f32),
            pltpu.VMEM((16, LANES), f32),
            pltpu.VMEM((16 + 2 * PAD, LANES), f32),
            pltpu.VMEM((16 + 2 * PAD, LANES), f32),
            pltpu.VMEM((3, fh + 2 * PAD, ext_w), f32),
            pltpu.VMEM((fh, LANES), f32),
            pltpu.VMEM((fh + 2 * PAD, LANES), f32),
            pltpu.VMEM((fh + 2 * PAD, LANES), f32),
            pltpu.VMEM((nslots * 8, tw), f32),
            pltpu.VMEM((3, 8, LANES), f32),
            pltpu.VMEM((3 * nrow, 8, LANES), f32),
            pltpu.VMEM((8, ext_w), f32),
            pltpu.VMEM((fh, tw), f32),
            pltpu.VMEM((fh, tw), jnp.int32),
            pltpu.VMEM((fh, tw), jnp.int32),
            pltpu.SMEM(manning.shape, f32),
            pltpu.SMEM(nest_map.shape, jnp.int32),
            pltpu.SemaphoreType.DMA((16,)),
            pltpu.SemaphoreType.DMA((16,)),
            pltpu.SemaphoreType.DMA((3,)),
            pltpu.SemaphoreType.DMA((3 * nrow,)),
            pltpu.SemaphoreType.DMA((9,)),
        ],
        compiler_params=pltpu.CompilerParams(
            collective_id=0, has_side_effects=True, vmem_limit_bytes=60 * 1024 * 1024
        ),
    )(*args)
    outs = [pltpu.with_memory_space_constraint(x, pltpu.VMEM) for x in outs]
    return pl.pallas_call(
        deliver,
        out_shape=shapes,
        in_specs=[vmem] * 3,
        out_specs=(hbm, hbm, hbm),
        scratch_shapes=[pltpu.SemaphoreType.DMA((3,))],
    )(*outs)


def solution(mesh):
    in_specs = (
        P("rows", "cols"),
        P(None, "rows", "cols"),
        P("rows", "cols"),
        P("rows", "cols"),
        P("rows", "cols"),
        P("rows", "cols"),
        P("rows", "cols"),
        P(),
        P(),
    )
    out_specs = (P("rows", "cols"), P("rows", "cols"), P(None, "rows", "cols"))
    body = functools.partial(per_device, mesh.shape["rows"], mesh.shape["cols"])
    return jax.shard_map(body, mesh=mesh, in_specs=in_specs, out_specs=out_specs, check_vma=False)
```
